32 devices in a mesh: grp: 2 (over x), st: 16 (over z, y, core).
Axes of the slice: x: 2, y: 2, z: 4, core: 2. Of those that a mesh axis runs over, the one named last changes fastest.
Arguments:
- ensemble: bfloat16 [128, 32768], P('st', 'grp'), parts along dimension 1, may hold values from -6 to 6
- obs_value: float32 [8, 4096], P('grp'), parts along dimension 0, may hold values from -6 to 6
- obs_spread: float32 [8, 4096], P('grp'), parts along dimension 0, may hold values from 0.5 to 2
- obs_noise: bfloat16 [8, 128, 4096], P('grp'), parts along dimension 0, may hold values from -5 to 5
- owner: int32 [8], P('grp'), parts along dimension 0, may hold values from 0 to 15, as said below
- obs_local: int32 [8, 4096], P('grp'), parts along dimension 0, may hold values from 0 to 1023, as said below
- loc_count: int32 [4, 128], P(None, ('grp', 'st')), parts along dimension 1, may hold values from 1 to 4, as said below
- loc_obs: int32 [4, 128, 4], P(None, ('grp', 'st')), parts along dimension 1, may hold values from 0 to 15
- loc_shift: int32 [4, 128, 4], P(None, ('grp', 'st')), parts along dimension 1, may hold values from 0 to 255
Outputs:
- analysis: bfloat16 [128, 32768], P(None, ('grp', 'st')), parts along dimension 1
The draws below stay inside these ranges and needn't reach their ends.
There are 2 independent parts, one for each index of `grp`. The reference program is written for one: setup_inputs(seed, part) draws one part's arguments, and reference() takes and returns one part's arrays. A program takes and returns all parts, laid end to end along the dimension named above; each array names one. Nothing has to cross between parts.
Inputs may be any that keep to these rules, and one draw needn't show every extreme that they name: owner[b] is drawn uniformly over the regions. `obs_local`: observation block k of a batch observes variables k * (64) .. (k + 1) * 64 - 1 of the region. loc_count[b, i] slots of loc_obs and loc_shift are used for state block i; the others are ignored. Every state block has at least 1; the first state block of the observed region has 4. Regions are busy or quiet as a whole.
All inputs are finite; a program needn't handle non-finite values.
Results may differ from the reference program's by a relative error of at most 0.009.
Values may be sent and summed in bfloat16 or wider, within the bound.
A program may use at most 128 MiB of HBM per device.

```python
import math
import jax
import jax.numpy as jnp
from jax import lax

M = 128
S_DEV = 1024
BLK = 256
OBS_B = 4096
NB = 4
KMAX = 4
NSTATE = 16384
NBLK = 64
BLK_DEV = 4
NOB = 16


def owner_helper(key):
    groups = NBLK // BLK_DEV
    return jax.random.randint(jax.random.fold_in(key, 5), (NB,), 0, groups).astype(jnp.int32)


def draw_owner(key, part):
    return owner_helper(key)


def draw_obs_local(key, part):
    span = S_DEV // NOB
    within = jax.random.randint(jax.random.fold_in(key, 23), (NB, NOB, BLK), 0, span)
    base = (jnp.arange(NOB, dtype=jnp.int32) * span)[None, :, None]
    return (within + base).reshape(NB, OBS_B).astype(jnp.int32)


def draw_loc_count(key, part):
    groups = NBLK // BLK_DEV
    owners = owner_helper(key)
    first_key, second_key = jax.random.split(jax.random.fold_in(key, 17))
    busy = jax.random.randint(first_key, (NB, groups), 0, 4) == 0
    busy = jnp.repeat(busy, BLK_DEV, axis=1)
    many = jax.random.randint(second_key, (NB, NBLK), 2, KMAX + 1)
    counts = jnp.where(busy, many, 1)
    first_block = (owners * BLK_DEV)[:, None]
    counts = jnp.where(jnp.arange(NBLK, dtype=jnp.int32)[None, :] == first_block, KMAX, counts)
    return counts.astype(jnp.int32)


def plant(values, key, least, largest):
    shape = values.shape
    place = [jax.random.randint(jax.random.fold_in(key, axis), (), 0, shape[axis]) for axis in range(len(shape))]
    values = values.at[tuple(place)].set(least)
    longest = shape.index(max(shape))
    place[longest] = (place[longest] + 1) % shape[longest]
    return values.at[tuple(place)].set(largest)


def level_of(rng, shape, shards, smallest, largest):
    factor_of = 1.0
    for dim, shards_of in shards:
        heights = jax.random.uniform(jax.random.fold_in(jax.random.fold_in(rng, 6), dim), (shards_of,), jnp.float32, smallest / len(shards), largest / len(shards))
        factor_of = factor_of * jnp.repeat(jnp.exp(heights), shape[dim] // shards_of).reshape((-1,) + (1,) * (len(shape) - 1 - dim))
    return factor_of


def gaussian(key, extent, deviation, bound, cuts=(), held_as=jnp.bfloat16):
    values = jax.random.normal(key, extent, jnp.float32) * deviation
    if len(cuts) > 0:
        values = level_of(key, extent, cuts, -0.22, 0.18) * values
    return jnp.clip(values, min=-bound, max=bound).astype(held_as)


def setup_inputs(seed: int = 0, part: int = 0) -> dict:
    key_list = jax.random.split(jax.random.key(seed), 10)
    part_keys = jax.random.split(jax.random.fold_in(key_list[9], part), 10)
    return {
        "ensemble": gaussian(part_keys[0], (M, NSTATE), 1.0, 6.0, ((0, 16),)),
        "obs_value": gaussian(part_keys[1], (NB, OBS_B), 1.0, 6.0, (), jnp.float32),
        "obs_spread": jnp.clip(jnp.exp(jax.random.uniform(part_keys[2], (NB, OBS_B), jnp.float32, math.log(0.5), math.log(2.0))), 0.5, 2.0),
        "obs_noise": gaussian(part_keys[3], (NB, M, OBS_B), 1.0, 5.0),
        "owner": draw_owner(jax.random.fold_in(jax.random.fold_in(key_list[9], part), 71), part),
        "obs_local": draw_obs_local(jax.random.fold_in(jax.random.fold_in(key_list[9], part), 71), part),
        "loc_count": draw_loc_count(jax.random.fold_in(jax.random.fold_in(key_list[9], part), 71), part),
        "loc_obs": plant(jax.random.randint(part_keys[7], (NB, NBLK, KMAX), 0, NOB), jax.random.fold_in(part_keys[7], 1), 0, NOB - 1).astype(jnp.int32),
        "loc_shift": plant(jax.random.randint(part_keys[8], (NB, NBLK, KMAX), 0, BLK), jax.random.fold_in(part_keys[8], 1), 0, BLK - 1).astype(jnp.int32),
    }


inflation = 4.0

def gains(rows, value, spread, noise):
    scale = math.sqrt(inflation) * spread
    center = lax.optimization_barrier(jnp.mean(rows, axis=0, keepdims=True))
    norm_rows = (rows - center) / (scale * math.sqrt(M - 1.0))
    misfit = (value + scale * noise.astype(jnp.float32) - rows) / scale
    count = rows.shape[1] // BLK
    s_blocks = norm_rows.reshape(M, count, BLK).transpose(1, 0, 2)
    d_blocks = misfit.reshape(M, count, BLK).transpose(1, 0, 2)
    system = jnp.eye(M, dtype=jnp.float32)[None] + jnp.einsum('kmo,kno->kmn', s_blocks, s_blocks, precision=lax.Precision.HIGHEST)
    right = jnp.einsum('kmo,kno->kmn', s_blocks, d_blocks, precision=lax.Precision.HIGHEST)
    lower = jnp.linalg.cholesky(system)
    inner = jax.scipy.linalg.solve_triangular(lower, right, lower=True)
    solved = jax.scipy.linalg.solve_triangular(lower, inner, lower=True, trans=1)
    return (solved / math.sqrt(M - 1.0)).astype(jnp.bfloat16)

def taper_of(shift):
    offsets = jnp.arange(BLK, dtype=jnp.float32)[None, :] - shift.astype(jnp.float32)[:, None]
    ratio = offsets / (BLK / 4.0)
    return 1.0 / (1.0 + ratio * ratio)

def reference(ensemble, obs_value, obs_spread, obs_noise, owner, obs_local, loc_count, loc_obs, loc_shift):
    groups = NSTATE // S_DEV
    state = ensemble.astype(jnp.float32)
    for batch in range(NB):
        start = (owner[batch] * S_DEV).astype(jnp.int32)
        region = lax.dynamic_slice_in_dim(state, start, S_DEV, 1)
        rows = jnp.take(region, obs_local[batch], axis=1)
        weights = gains(rows, obs_value[batch], obs_spread[batch], obs_noise[batch])
        center = lax.optimization_barrier(jnp.mean(state, axis=0, keepdims=True))
        anomalies = (state - center).astype(jnp.bfloat16)
        counts = loc_count[batch]
        pairs = loc_obs[batch]
        shifts = loc_shift[batch]

        def one_group(index):
            first = (index * S_DEV).astype(jnp.int32)
            firstblk = (index * BLK_DEV).astype(jnp.int32)
            cols = lax.dynamic_slice_in_dim(anomalies, first, S_DEV, 1).reshape(M, BLK_DEV, BLK).astype(jnp.float32)
            cnt = lax.dynamic_slice_in_dim(counts, firstblk, BLK_DEV, 0)
            idx = lax.dynamic_slice_in_dim(pairs, firstblk, BLK_DEV, 0)
            shf = lax.dynamic_slice_in_dim(shifts, firstblk, BLK_DEV, 0)
            total = jnp.zeros((M, BLK_DEV, BLK), jnp.float32)
            for slot in range(KMAX):
                picked = jnp.take(weights, idx[:, slot], axis=0).astype(jnp.float32)
                term = jnp.einsum('ilm,liv->miv', picked, cols)
                factor = jnp.where((cnt > slot)[:, None], taper_of(shf[:, slot]), 0.0)
                total = total + term * factor[None]
            return total.reshape(M, S_DEV)
        increments = lax.map(one_group, jnp.arange(groups, dtype=jnp.int32))
        state = state + increments.transpose(1, 0, 2).reshape(M, NSTATE)
    return state.astype(jnp.bfloat16)
```

```python
import functools
import math

import jax
import jax.numpy as jnp
from jax import lax
from jax.experimental import pallas as pl
from jax.experimental.pallas import tpu as pltpu
from jax.sharding import PartitionSpec as P

M = 128
BLK = 256
NB = 4
KMAX = 4
SPAN = 64
PAIR = 2 * SPAN
REGION = 1024
BLOCKS = REGION // BLK
NOB = REGION // SPAN
ENTRY = 1 + 2 * KMAX
TABLE = NB * BLOCKS * ENTRY
ROOT = math.sqrt(M - 1.0)
inflation = 4.0
HIGHEST = lax.Precision.HIGHEST
NT = (((1,), (1,)), ((), ()))


def prepare(value_ref, spread_ref, local_ref, noise_ref, rhs_ref, weight_ref):
    def one(k, carry):
        cols = pl.ds(pl.multiple_of(k * BLK, BLK), BLK)
        inv = 1.0 / (math.sqrt(inflation) * spread_ref[0, :, cols])
        var = lax.broadcasted_iota(jnp.int32, (SPAN, BLK), 0) + k * SPAN
        hit = var == local_ref[0, :, cols]
        placed = jnp.where(hit, inv, 0.0)
        high = placed.astype(jnp.bfloat16)
        low = (placed - high.astype(jnp.float32)).astype(jnp.bfloat16)
        noise = noise_ref[0, :, cols]
        summed = lax.dot_general(high, noise, NT, preferred_element_type=jnp.float32)
        summed += lax.dot_general(low, noise, NT, preferred_element_type=jnp.float32)
        square = placed * inv
        weight = jnp.sum(square, axis=1, keepdims=True)
        summed += jnp.sum(square * value_ref[0, :, cols], axis=1, keepdims=True)
        rows = pl.ds(pl.multiple_of(k * SPAN, SPAN), SPAN)
        rhs_ref[0, rows, :] = summed
        weight_ref[0, rows, :] = jnp.broadcast_to(weight, (SPAN, M))
        return carry

    lax.fori_loop(0, NOB, one, 0)


def assimilate(table_ref, owned_ref, mine_ref, rhs_ref, weight_ref, out_ref,
               state, taper, system, right, factor, weights, anoms):
    lane = lax.broadcasted_iota(jnp.int32, (SPAN, PAIR), 1)
    first = lane < SPAN
    chunks = REGION // 128

    def bring_owned(c, carry):
        at = pl.multiple_of(c * 128, 128)
        state[pl.ds(at, 128), :] = owned_ref[:, pl.ds(at, 128)].astype(jnp.float32).T
        return carry

    lax.fori_loop(0, NB * chunks, bring_owned, 0)

    def bring_mine(c, carry):
        at = pl.multiple_of(c * 128, 128)
        state[pl.ds(NB * REGION + at, 128), :] = mine_ref[:, pl.ds(at, 128)].astype(jnp.float32).T
        return carry

    lax.fori_loop(0, chunks, bring_mine, 0)

    offset = (lax.broadcasted_iota(jnp.int32, (2 * BLK, M), 0) - BLK).astype(jnp.float32)
    ratio = offset / (BLK / 4.0)
    taper[...] = 1.0 / (1.0 + ratio * ratio)

    for batch in range(NB):

        def build(p, carry):
            rows = pl.ds(pl.multiple_of(p * PAIR, PAIR), PAIR)
            x = state[pl.ds(pl.multiple_of(batch * REGION + p * PAIR, PAIR), PAIR), :]
            anom = x - jnp.mean(x, axis=1, keepdims=True)
            weight = weight_ref[batch, rows, :]
            live = weight > 0.0
            inverse = jnp.where(live, lax.rsqrt(jnp.where(live, weight, 1.0)), 0.0)
            scaled = anom * (weight * inverse * (1.0 / ROOT))
            factor[rows, :] = scaled
            right[rows, :] = (rhs_ref[batch, rows, :] - weight * x) * (inverse * (1.0 / ROOT))
            gram = lax.dot_general(scaled, scaled, NT, precision=HIGHEST, preferred_element_type=jnp.float32)
            row = lax.broadcasted_iota(jnp.int32, (SPAN, PAIR), 0)
            eye = jnp.where(row == jnp.where(first, lane, lane - SPAN), 1.0, 0.0)
            packed = jnp.where(first, gram[:SPAN], gram[SPAN:]) + eye
            system[pl.ds(pl.multiple_of(p * SPAN, SPAN), SPAN), :] = packed
            return carry

        lax.fori_loop(0, NOB // 2, build, 0)

        def eliminate(j, carry):
            pick = jnp.where(first, j, j + SPAN)
            hit = lane == pick
            for p in range(NOB // 2):
                full = system[p * SPAN:(p + 1) * SPAN, :]
                row = system[pl.ds(p * SPAN + j, 1), :]
                column = jnp.take_along_axis(full, pick, axis=1)
                rows8 = jnp.broadcast_to(row, (8, PAIR))
                pivot = jnp.take_along_axis(rows8, pick[:8], axis=1)
                inv = 1.0 / pivot
                scaled = jnp.where(hit[:8], inv, rows8 * inv)[:1]
                system[p * SPAN:(p + 1) * SPAN, :] = jnp.where(hit, 0.0, full) - column * scaled
                system[pl.ds(p * SPAN + j, 1), :] = scaled
            return carry

        lax.fori_loop(0, SPAN, eliminate, 0)

        def finish(p, carry):
            rows = pl.ds(pl.multiple_of(p * PAIR, PAIR), PAIR)
            packed = system[pl.ds(pl.multiple_of(p * SPAN, SPAN), SPAN), :]
            whole = jnp.concatenate([jnp.where(first, packed, 0.0), jnp.where(first, 0.0, packed)], axis=0)
            solved = jnp.dot(whole, right[rows, :], precision=HIGHEST, preferred_element_type=jnp.float32)
            left = factor[rows, :].T
            lanes = lax.broadcasted_iota(jnp.int32, (M, PAIR), 1) < SPAN
            for half, keep in enumerate((lanes, jnp.logical_not(lanes))):
                made = jnp.dot(jnp.where(keep, left, 0.0), solved, precision=HIGHEST, preferred_element_type=jnp.float32)
                weights[2 * p + half] = made.astype(jnp.bfloat16)
            return carry

        lax.fori_loop(0, NOB // 2, finish, 0)

        def update(index, carry):
            region = batch + 1 + index // BLOCKS
            block = index % BLOCKS
            base = ((region * NB + batch) * BLOCKS + block) * ENTRY
            rows = pl.ds(pl.multiple_of((batch + 1) * REGION + index * BLK, BLK), BLK)
            x = state[rows, :]
            anoms[...] = (x - jnp.mean(x, axis=1, keepdims=True)).astype(jnp.bfloat16)

            def slot(j, carry):
                k = table_ref[base + 1 + j]
                shift = table_ref[base + 1 + KMAX + j]
                term = jnp.dot(anoms[...], weights[k], preferred_element_type=jnp.float32)
                state[rows, :] += term * taper[pl.ds(BLK - shift, BLK), :]
                return carry

            lax.fori_loop(0, table_ref[base], slot, 0)
            return carry

        lax.fori_loop(0, (NB - batch) * BLOCKS, update, 0)

    def leave(c, carry):
        at = pl.multiple_of(c * 128, 128)
        out_ref[:, pl.ds(at, 128)] = state[pl.ds(NB * REGION + at, 128), :].T.astype(jnp.bfloat16)
        return carry

    lax.fori_loop(0, chunks, leave, 0)


def shards(
    ensemble, obs_value, obs_spread, obs_noise, owner, obs_local, loc_count, loc_obs, loc_shift
):
    members = ensemble.shape[0]
    mine = lax.all_to_all(ensemble, "st", split_axis=1, concat_axis=0, tiled=True)
    table = jnp.concatenate([loc_count[:, :, None], loc_obs, loc_shift], axis=2)
    pad = -(-TABLE // (members * 128)) * 128
    flat = jnp.pad(table.reshape(TABLE).astype(jnp.bfloat16), (0, members * pad - TABLE))
    parts = [lax.dynamic_slice_in_dim(ensemble, owner[b] * REGION, REGION, 1) for b in range(NB)]
    sent = jnp.concatenate(parts + [flat.reshape(members, pad)], axis=1)
    got = lax.all_gather(sent, "st", axis=0, tiled=True)
    owned = got[:, :NB * REGION]
    tables = got[:, NB * REGION:].reshape(-1, members * pad)[:, :TABLE]
    picked = [lax.dynamic_slice_in_dim(tables, owner[b], 1, 0).reshape(TABLE) for b in range(NB)]
    all_tables = jnp.concatenate(
        [jnp.concatenate(picked).astype(jnp.int32), table.reshape(TABLE)]
    )

    rhs, weight = pl.pallas_call(
        prepare,
        grid=(NB,),
        in_specs=[
            pl.BlockSpec((1, 1, NOB * BLK), lambda b: (b, 0, 0)),
            pl.BlockSpec((1, 1, NOB * BLK), lambda b: (b, 0, 0)),
            pl.BlockSpec((1, 1, NOB * BLK), lambda b: (b, 0, 0)),
            pl.BlockSpec((1, M, NOB * BLK), lambda b: (b, 0, 0)),
        ],
        out_specs=[pl.BlockSpec((1, REGION, M), lambda b: (b, 0, 0))] * 2,
        out_shape=[jax.ShapeDtypeStruct((NB, REGION, M), jnp.float32)] * 2,
        compiler_params=pltpu.CompilerParams(vmem_limit_bytes=16 << 20),
        cost_estimate=pl.CostEstimate(flops=1 << 29, bytes_accessed=8 << 20, transcendentals=0),
        name="prepare",
    )(obs_value[:, None], obs_spread[:, None], obs_local[:, None], obs_noise)

    vmem = pl.BlockSpec(memory_space=pltpu.VMEM)
    return pl.pallas_call(
        assimilate,
        in_specs=[pl.BlockSpec(memory_space=pltpu.SMEM)] + [vmem] * 4,
        out_specs=vmem,
        out_shape=jax.ShapeDtypeStruct((M, REGION), jnp.bfloat16),
        scratch_shapes=[
            pltpu.VMEM(((NB + 1) * REGION, M), jnp.float32),
            pltpu.VMEM((2 * BLK, M), jnp.float32),
            pltpu.VMEM((NOB // 2 * SPAN, PAIR), jnp.float32),
            pltpu.VMEM((REGION, M), jnp.float32),
            pltpu.VMEM((REGION, M), jnp.float32),
            pltpu.VMEM((NOB, M, M), jnp.bfloat16),
            pltpu.VMEM((BLK, M), jnp.bfloat16),
        ],
        compiler_params=pltpu.CompilerParams(vmem_limit_bytes=40 << 20),
        name="assimilate",
    )(all_tables, owned, mine, rhs, weight)


def solution(mesh):
    placed = (
        P("st", "grp"),
        P("grp", None),
        P("grp", None),
        P("grp", None, None),
        P("grp"),
        P("grp", None),
        P(None, ("grp", "st")),
        P(None, ("grp", "st"), None),
        P(None, ("grp", "st"), None),
    )
    return jax.shard_map(
        shards, mesh=mesh, in_specs=placed, out_specs=P(None, ("grp", "st")), check_vma=False
    )
```

```python
import functools
import math

import jax
import jax.numpy as jnp
from jax import lax
from jax.experimental import pallas as pl
from jax.experimental.pallas import tpu as pltpu
from jax.sharding import PartitionSpec as P

M = 128
BLK = 256
NB = 4
KMAX = 4
SPAN = 64
PAIR = 2 * SPAN
REGION = 1024
BLOCKS = REGION // BLK
NOB = REGION // SPAN
ENTRY = 1 + 2 * KMAX
TABLE = NB * BLOCKS * ENTRY
ROOT = math.sqrt(M - 1.0)
inflation = 4.0
HIGHEST = lax.Precision.HIGHEST
NT = (((1,), (1,)), ((), ()))


def prepare(value_ref, spread_ref, local_ref, noise_ref, rhs_ref, weight_ref):
    def one(k, carry):
        cols = pl.ds(pl.multiple_of(k * BLK, BLK), BLK)
        inv = 1.0 / (math.sqrt(inflation) * spread_ref[0, :, cols])
        var = lax.broadcasted_iota(jnp.int32, (SPAN, BLK), 0) + k * SPAN
        hit = var == local_ref[0, :, cols]
        placed = jnp.where(hit, inv, 0.0)
        high = placed.astype(jnp.bfloat16)
        low = (placed - high.astype(jnp.float32)).astype(jnp.bfloat16)
        noise = noise_ref[0, :, cols]
        summed = lax.dot_general(high, noise, NT, preferred_element_type=jnp.float32)
        summed += lax.dot_general(low, noise, NT, preferred_element_type=jnp.float32)
        square = placed * inv
        weight = jnp.sum(square, axis=1, keepdims=True)
        summed += jnp.sum(square * value_ref[0, :, cols], axis=1, keepdims=True)
        rows = pl.ds(pl.multiple_of(k * SPAN, SPAN), SPAN)
        rhs_ref[0, rows, :] = summed
        weight_ref[0, rows, :] = jnp.broadcast_to(weight, (SPAN, M))
        return carry

    lax.fori_loop(0, NOB, one, 0)


def assimilate(table_ref, owned_ref, mine_ref, rhs_ref, weight_ref, out_ref,
               state, taper, system, right, factor, weights, anoms):
    lane = lax.broadcasted_iota(jnp.int32, (SPAN, PAIR), 1)
    first = lane < SPAN
    chunks = REGION // 128

    def bring_owned(c, carry):
        at = pl.multiple_of(c * 128, 128)
        state[pl.ds(at, 128), :] = owned_ref[:, pl.ds(at, 128)].astype(jnp.float32).T
        return carry

    lax.fori_loop(0, NB * chunks, bring_owned, 0, unroll=4)

    def bring_mine(c, carry):
        at = pl.multiple_of(c * 128, 128)
        state[pl.ds(NB * REGION + at, 128), :] = mine_ref[:, pl.ds(at, 128)].astype(jnp.float32).T
        return carry

    lax.fori_loop(0, chunks, bring_mine, 0, unroll=4)

    offset = (lax.broadcasted_iota(jnp.int32, (2 * BLK, M), 0) - BLK).astype(jnp.float32)
    ratio = offset / (BLK / 4.0)
    taper[...] = 1.0 / (1.0 + ratio * ratio)

    for batch in range(NB):

        def build(p, carry):
            rows = pl.ds(pl.multiple_of(p * PAIR, PAIR), PAIR)
            x = state[pl.ds(pl.multiple_of(batch * REGION + p * PAIR, PAIR), PAIR), :]
            anom = x - jnp.mean(x, axis=1, keepdims=True)
            weight = weight_ref[batch, rows, :]
            live = weight > 0.0
            inverse = jnp.where(live, lax.rsqrt(jnp.where(live, weight, 1.0)), 0.0)
            scaled = anom * (weight * inverse * (1.0 / ROOT))
            factor[rows, :] = scaled
            right[rows, :] = (rhs_ref[batch, rows, :] - weight * x) * (inverse * (1.0 / ROOT))
            gram = lax.dot_general(scaled, scaled, NT, precision=HIGHEST, preferred_element_type=jnp.float32)
            row = lax.broadcasted_iota(jnp.int32, (SPAN, PAIR), 0)
            eye = jnp.where(row == jnp.where(first, lane, lane - SPAN), 1.0, 0.0)
            packed = jnp.where(first, gram[:SPAN], gram[SPAN:]) + eye
            system[pl.ds(pl.multiple_of(p * SPAN, SPAN), SPAN), :] = packed
            return carry

        lax.fori_loop(0, NOB // 2, build, 0, unroll=4)

        def eliminate(j, carry):
            pick = jnp.where(first, j, j + SPAN)
            hit = lane == pick
            pairs = range(NOB // 2)
            fulls = [system[p * SPAN:(p + 1) * SPAN, :] for p in pairs]
            rows = system[pl.ds(j, NOB // 2, stride=SPAN), :]
            inv = 1.0 / jnp.take_along_axis(rows, pick[:NOB // 2], axis=1)
            scaled = jnp.where(hit[:NOB // 2], inv, rows * inv)
            columns = [jnp.take_along_axis(full, pick, axis=1) for full in fulls]
            made = [
                jnp.where(hit, 0.0, fulls[p]) - columns[p] * scaled[p:p + 1] for p in pairs
            ]
            for p in pairs:
                system[p * SPAN:(p + 1) * SPAN, :] = made[p]
            system[pl.ds(j, NOB // 2, stride=SPAN), :] = scaled
            return carry

        lax.fori_loop(0, SPAN, eliminate, 0)

        def finish(p, carry):
            rows = pl.ds(pl.multiple_of(p * PAIR, PAIR), PAIR)
            packed = system[pl.ds(pl.multiple_of(p * SPAN, SPAN), SPAN), :]
            whole = jnp.concatenate([jnp.where(first, packed, 0.0), jnp.where(first, 0.0, packed)], axis=0)
            solved = jnp.dot(whole, right[rows, :], precision=HIGHEST, preferred_element_type=jnp.float32)
            left = factor[rows, :].T
            lanes = lax.broadcasted_iota(jnp.int32, (M, PAIR), 1) < SPAN
            for half, keep in enumerate((lanes, jnp.logical_not(lanes))):
                made = jnp.dot(jnp.where(keep, left, 0.0), solved, precision=HIGHEST, preferred_element_type=jnp.float32)
                weights[2 * p + half] = made.astype(jnp.bfloat16)
            return carry

        lax.fori_loop(0, NOB // 2, finish, 0, unroll=4)

        def update(index, carry):
            region = batch + 1 + index // BLOCKS
            block = index % BLOCKS
            base = ((region * NB + batch) * BLOCKS + block) * ENTRY
            rows = pl.ds(pl.multiple_of((batch + 1) * REGION + index * BLK, BLK), BLK)
            x = state[rows, :]
            anoms[...] = (x - jnp.mean(x, axis=1, keepdims=True)).astype(jnp.bfloat16)

            def slot(j, carry):
                k = table_ref[base + 1 + j]
                shift = table_ref[base + 1 + KMAX + j]
                term = jnp.dot(anoms[...], weights[k], preferred_element_type=jnp.float32)
                state[rows, :] += term * taper[pl.ds(BLK - shift, BLK), :]
                return carry

            lax.fori_loop(0, table_ref[base], slot, 0)
            return carry

        lax.fori_loop(0, (NB - batch) * BLOCKS, update, 0)

    def leave(c, carry):
        at = pl.multiple_of(c * 128, 128)
        out_ref[:, pl.ds(at, 128)] = state[pl.ds(NB * REGION + at, 128), :].T.astype(jnp.bfloat16)
        return carry

    lax.fori_loop(0, chunks, leave, 0, unroll=4)


def shards(
    ensemble, obs_value, obs_spread, obs_noise, owner, obs_local, loc_count, loc_obs, loc_shift
):
    members = ensemble.shape[0]
    mine = lax.all_to_all(ensemble, "st", split_axis=1, concat_axis=0, tiled=True)
    table = jnp.concatenate([loc_count[:, :, None], loc_obs, loc_shift], axis=2)
    pad = -(-TABLE // (members * 128)) * 128
    flat = jnp.pad(table.reshape(TABLE).astype(jnp.bfloat16), (0, members * pad - TABLE))
    parts = [lax.dynamic_slice_in_dim(ensemble, owner[b] * REGION, REGION, 1) for b in range(NB)]
    sent = jnp.concatenate(parts + [flat.reshape(members, pad)], axis=1)
    got = lax.all_gather(sent, "st", axis=0, tiled=True)
    owned = got[:, :NB * REGION]
    tables = got[:, NB * REGION:].reshape(-1, members * pad)[:, :TABLE]
    picked = [lax.dynamic_slice_in_dim(tables, owner[b], 1, 0).reshape(TABLE) for b in range(NB)]
    all_tables = jnp.concatenate(
        [jnp.concatenate(picked).astype(jnp.int32), table.reshape(TABLE)]
    )

    rhs, weight = pl.pallas_call(
        prepare,
        grid=(NB,),
        in_specs=[
            pl.BlockSpec((1, 1, NOB * BLK), lambda b: (b, 0, 0)),
            pl.BlockSpec((1, 1, NOB * BLK), lambda b: (b, 0, 0)),
            pl.BlockSpec((1, 1, NOB * BLK), lambda b: (b, 0, 0)),
            pl.BlockSpec((1, M, NOB * BLK), lambda b: (b, 0, 0)),
        ],
        out_specs=[pl.BlockSpec((1, REGION, M), lambda b: (b, 0, 0))] * 2,
        out_shape=[jax.ShapeDtypeStruct((NB, REGION, M), jnp.float32)] * 2,
        compiler_params=pltpu.CompilerParams(vmem_limit_bytes=16 << 20),
        cost_estimate=pl.CostEstimate(flops=1 << 29, bytes_accessed=8 << 20, transcendentals=0),
        name="prepare",
    )(obs_value[:, None], obs_spread[:, None], obs_local[:, None], obs_noise)

    vmem = pl.BlockSpec(memory_space=pltpu.VMEM)
    return pl.pallas_call(
        assimilate,
        in_specs=[pl.BlockSpec(memory_space=pltpu.SMEM)] + [vmem] * 4,
        out_specs=vmem,
        out_shape=jax.ShapeDtypeStruct((M, REGION), jnp.bfloat16),
        scratch_shapes=[
            pltpu.VMEM(((NB + 1) * REGION, M), jnp.float32),
            pltpu.VMEM((2 * BLK, M), jnp.float32),
            pltpu.VMEM((NOB // 2 * SPAN, PAIR), jnp.float32),
            pltpu.VMEM((REGION, M), jnp.float32),
            pltpu.VMEM((REGION, M), jnp.float32),
            pltpu.VMEM((NOB, M, M), jnp.bfloat16),
            pltpu.VMEM((BLK, M), jnp.bfloat16),
        ],
        compiler_params=pltpu.CompilerParams(vmem_limit_bytes=40 << 20),
        name="assimilate",
    )(all_tables, owned, mine, rhs, weight)


def solution(mesh):
    placed = (
        P("st", "grp"),
        P("grp", None),
        P("grp", None),
        P("grp", None, None),
        P("grp"),
        P("grp", None),
        P(None, ("grp", "st")),
        P(None, ("grp", "st"), None),
        P(None, ("grp", "st"), None),
    )
    return jax.shard_map(
        shards, mesh=mesh, in_specs=placed, out_specs=P(None, ("grp", "st")), check_vma=False
    )
```

```python
import functools
import math

import jax
import jax.numpy as jnp
from jax import lax
from jax.experimental import pallas as pl
from jax.experimental.pallas import tpu as pltpu
from jax.sharding import PartitionSpec as P

M = 128
BLK = 256
NB = 4
KMAX = 4
SPAN = 64
PAIR = 2 * SPAN
REGION = 1024
BLOCKS = REGION // BLK
NOB = REGION // SPAN
ENTRY = 1 + 2 * KMAX
TABLE = NB * BLOCKS * ENTRY
ROOT = math.sqrt(M - 1.0)
inflation = 4.0
HIGHEST = lax.Precision.HIGHEST
MESH = pl.DeviceIdType.MESH
NT = (((1,), (1,)), ((), ()))


def exchange(ways, value_ref, spread_ref, local_ref, noise_ref, sent_ref, share_ref,
             got_ref, mine_ref, rhs_ref, weight_ref, send_sem, recv_sem, part_send, part_recv):
    me = lax.axis_index("st")
    partner = me + 1 - 2 * lax.rem(me, 2)
    half = ways // 2

    barrier = pltpu.get_barrier_semaphore()

    def greet(step, carry):
        peer = lax.rem(me + step, ways)
        pl.semaphore_signal(barrier, inc=1, device_id={"st": peer}, device_id_type=MESH)
        return carry

    lax.fori_loop(1, ways, greet, 0)
    pl.semaphore_wait(barrier, ways - 1)

    def whole(step):
        peer = lax.rem(me + 2 * step, ways)
        return pltpu.make_async_remote_copy(
            src_ref=sent_ref, dst_ref=got_ref.at[me], send_sem=send_sem.at[step],
            recv_sem=recv_sem.at[me], device_id={"st": peer}, device_id_type=MESH)

    def across(source, slot, src_ref):
        return pltpu.make_async_remote_copy(
            src_ref=src_ref, dst_ref=got_ref.at[source], send_sem=send_sem.at[slot],
            recv_sem=recv_sem.at[source], device_id={"st": partner}, device_id_type=MESH)

    def part(step):
        peer = lax.rem(me + step, ways)
        return pltpu.make_async_remote_copy(
            src_ref=share_ref.at[peer], dst_ref=mine_ref.at[me], send_sem=part_send.at[step],
            recv_sem=part_recv.at[me], device_id={"st": peer}, device_id_type=MESH)

    def arrived(source):
        pltpu.make_async_remote_copy(
            src_ref=sent_ref, dst_ref=got_ref.at[source], send_sem=send_sem.at[0],
            recv_sem=recv_sem.at[source], device_id={"st": partner}, device_id_type=MESH).wait_recv()

    def loop(low, high, body):
        lax.fori_loop(low, high, lambda i, c: (body(i), c)[1], 0)

    loop(1, half, lambda step: whole(step).start())
    across(me, 0, sent_ref).start()
    loop(1, ways, lambda step: part(step).start())
    got_ref[me] = sent_ref[...]
    mine_ref[me] = share_ref[me]

    def one(batch, k):
        cols = pl.ds(pl.multiple_of(k * BLK, BLK), BLK)
        inv = 1.0 / (math.sqrt(inflation) * spread_ref[batch, :, cols])
        var = lax.broadcasted_iota(jnp.int32, (SPAN, BLK), 0) + k * SPAN
        hit = var == local_ref[batch, :, cols]
        placed = jnp.where(hit, inv, 0.0)
        high = placed.astype(jnp.bfloat16)
        low = (placed - high.astype(jnp.float32)).astype(jnp.bfloat16)
        noise = noise_ref[batch, :, cols]
        summed = lax.dot_general(high, noise, NT, preferred_element_type=jnp.float32)
        summed += lax.dot_general(low, noise, NT, preferred_element_type=jnp.float32)
        square = placed * inv
        weight = jnp.sum(square, axis=1, keepdims=True)
        summed += jnp.sum(square * value_ref[batch, :, cols], axis=1, keepdims=True)
        rows = pl.ds(pl.multiple_of(k * SPAN, SPAN), SPAN)
        rhs_ref[batch, rows, :] = summed
        weight_ref[batch, rows, :] = jnp.broadcast_to(weight, (SPAN, M))

    def two(i, batch):
        one(batch, 2 * i)
        one(batch, 2 * i + 1)

    for batch in range(NB):
        loop(0, NOB // 2, lambda i: two(i, batch))

    def pass_on(step):
        source = lax.rem(me + ways - 2 * step, ways)
        arrived(source)
        across(source, half + step, got_ref.at[source]).start()

    loop(1, half, pass_on)

    def passed(step):
        arrived(lax.rem(partner + ways - 2 * step, ways))

    loop(0, half, passed)

    def settle(step):
        whole(step).wait_send()
        across(me, half + step, sent_ref).wait_send()

    loop(1, half, settle)
    across(me, 0, sent_ref).wait_send()

    def parted(step):
        part(step).wait_send()
        source = lax.rem(me + ways - step, ways)
        pltpu.make_async_remote_copy(
            src_ref=share_ref.at[me], dst_ref=mine_ref.at[source], send_sem=part_send.at[0],
            recv_sem=part_recv.at[source], device_id={"st": partner}, device_id_type=MESH).wait_recv()

    loop(1, ways, parted)


def assimilate(table_ref, owned_ref, mine_ref, rhs_ref, weight_ref, out_ref,
               state, taper, system, right, factor, weights, anoms):
    lane = lax.broadcasted_iota(jnp.int32, (SPAN, PAIR), 1)
    first = lane < SPAN
    chunks = REGION // 128

    def bring_owned(c, carry):
        at = pl.multiple_of(c * 128, 128)
        state[pl.ds(at, 128), :] = owned_ref[:, pl.ds(at, 128)].astype(jnp.float32).T
        return carry

    lax.fori_loop(0, NB * chunks, bring_owned, 0, unroll=4)

    def bring_mine(c, carry):
        at = pl.multiple_of(c * 128, 128)
        state[pl.ds(NB * REGION + at, 128), :] = mine_ref[:, pl.ds(at, 128)].astype(jnp.float32).T
        return carry

    lax.fori_loop(0, chunks, bring_mine, 0, unroll=4)

    offset = (lax.broadcasted_iota(jnp.int32, (2 * BLK, M), 0) - BLK).astype(jnp.float32)
    ratio = offset / (BLK / 4.0)
    taper[...] = 1.0 / (1.0 + ratio * ratio)

    for batch in range(NB):

        def build(p, carry):
            rows = pl.ds(pl.multiple_of(p * PAIR, PAIR), PAIR)
            x = state[pl.ds(pl.multiple_of(batch * REGION + p * PAIR, PAIR), PAIR), :]
            anom = x - jnp.mean(x, axis=1, keepdims=True)
            weight = weight_ref[batch, rows, :]
            live = weight > 0.0
            inverse = jnp.where(live, lax.rsqrt(jnp.where(live, weight, 1.0)), 0.0)
            scaled = anom * (weight * inverse * (1.0 / ROOT))
            factor[rows, :] = scaled
            right[rows, :] = (rhs_ref[batch, rows, :] - weight * x) * (inverse * (1.0 / ROOT))
            gram = lax.dot_general(scaled, scaled, NT, precision=HIGHEST, preferred_element_type=jnp.float32)
            row = lax.broadcasted_iota(jnp.int32, (SPAN, PAIR), 0)
            eye = jnp.where(row == jnp.where(first, lane, lane - SPAN), 1.0, 0.0)
            packed = jnp.where(first, gram[:SPAN], gram[SPAN:]) + eye
            system[pl.ds(pl.multiple_of(p * SPAN, SPAN), SPAN), :] = packed
            return carry

        lax.fori_loop(0, NOB // 2, build, 0, unroll=4)

        def eliminate(j, carry):
            pick = jnp.where(first, j, j + SPAN)
            hit = lane == pick
            pairs = range(NOB // 2)
            fulls = [system[p * SPAN:(p + 1) * SPAN, :] for p in pairs]
            rows = system[pl.ds(j, NOB // 2, stride=SPAN), :]
            inv = 1.0 / jnp.take_along_axis(rows, pick[:NOB // 2], axis=1)
            scaled = jnp.where(hit[:NOB // 2], inv, rows * inv)
            columns = [jnp.take_along_axis(full, pick, axis=1) for full in fulls]
            made = [
                jnp.where(hit, 0.0, fulls[p]) - columns[p] * scaled[p:p + 1] for p in pairs
            ]
            for p in pairs:
                system[p * SPAN:(p + 1) * SPAN, :] = made[p]
            system[pl.ds(j, NOB // 2, stride=SPAN), :] = scaled
            return carry

        lax.fori_loop(0, SPAN, eliminate, 0)

        def finish(p, carry):
            rows = pl.ds(pl.multiple_of(p * PAIR, PAIR), PAIR)
            packed = system[pl.ds(pl.multiple_of(p * SPAN, SPAN), SPAN), :]
            whole = jnp.concatenate([jnp.where(first, packed, 0.0), jnp.where(first, 0.0, packed)], axis=0)
            solved = jnp.dot(whole, right[rows, :], precision=HIGHEST, preferred_element_type=jnp.float32)
            left = factor[rows, :].T
            lanes = lax.broadcasted_iota(jnp.int32, (M, PAIR), 1) < SPAN
            for half, keep in enumerate((lanes, jnp.logical_not(lanes))):
                made = jnp.dot(jnp.where(keep, left, 0.0), solved, precision=HIGHEST, preferred_element_type=jnp.float32)
                weights[2 * p + half] = made.astype(jnp.bfloat16)
            return carry

        lax.fori_loop(0, NOB // 2, finish, 0, unroll=4)

        def update(index, carry):
            region = batch + 1 + index // BLOCKS
            block = index % BLOCKS
            base = ((region * NB + batch) * BLOCKS + block) * ENTRY
            rows = pl.ds(pl.multiple_of((batch + 1) * REGION + index * BLK, BLK), BLK)
            x = state[rows, :]
            anoms[...] = (x - jnp.mean(x, axis=1, keepdims=True)).astype(jnp.bfloat16)

            def slot(j, carry):
                k = table_ref[base + 1 + j]
                shift = table_ref[base + 1 + KMAX + j]
                term = jnp.dot(anoms[...], weights[k], preferred_element_type=jnp.float32)
                state[rows, :] += term * taper[pl.ds(BLK - shift, BLK), :]
                return carry

            lax.fori_loop(0, table_ref[base], slot, 0)
            return carry

        lax.fori_loop(0, (NB - batch) * BLOCKS, update, 0)

    def leave(c, carry):
        at = pl.multiple_of(c * 128, 128)
        out_ref[:, pl.ds(at, 128)] = state[pl.ds(NB * REGION + at, 128), :].T.astype(jnp.bfloat16)
        return carry

    lax.fori_loop(0, chunks, leave, 0, unroll=4)


def shards(
    ensemble, obs_value, obs_spread, obs_noise, owner, obs_local, loc_count, loc_obs, loc_shift
):
    members = ensemble.shape[0]
    ways = M // members
    table = jnp.concatenate([loc_count[:, :, None], loc_obs, loc_shift], axis=2)
    wide = REGION // 128
    base = NB * wide * members
    total = -(-(base + -(-TABLE // 128)) // 16) * 16
    flat = jnp.pad(table.reshape(TABLE).astype(jnp.bfloat16), (0, (total - base) * 128 - TABLE))

    def tall(x):
        return x.reshape(members, -1, 128).transpose(1, 0, 2).reshape(-1, 128)

    parts = [tall(lax.dynamic_slice_in_dim(ensemble, owner[b] * REGION, REGION, 1)) for b in range(NB)]
    sent = jnp.concatenate(parts + [flat.reshape(total - base, 128)], axis=0)
    share = tall(ensemble).reshape(ways, wide * members, 128)
    held = -(-wide * members // 16) * 16
    share = jnp.pad(share, ((0, 0), (0, held - wide * members), (0, 0)))

    vmem = pl.BlockSpec(memory_space=pltpu.VMEM)
    sums = jax.ShapeDtypeStruct((NB, REGION, M), jnp.float32)
    got, mine, rhs, weight = pl.pallas_call(
        functools.partial(exchange, ways),
        in_specs=[vmem] * 6,
        out_specs=[vmem] * 4,
        out_shape=[
            jax.ShapeDtypeStruct((ways, total, 128), jnp.bfloat16),
            jax.ShapeDtypeStruct((ways, held, 128), jnp.bfloat16),
            sums,
            sums,
        ],
        scratch_shapes=[pltpu.SemaphoreType.DMA((ways,))] * 4,
        compiler_params=pltpu.CompilerParams(
            collective_id=0, has_side_effects=True, vmem_limit_bytes=40 << 20
        ),
        name="exchange",
    )(obs_value[:, None], obs_spread[:, None], obs_local[:, None], obs_noise, sent, share)

    def across(x, count):
        return x[:, :count * members].reshape(ways, count, members, 128).transpose(0, 2, 1, 3).reshape(M, count * 128)

    owned = across(got, NB * wide)
    mine = across(mine, wide)
    tables = got[:, base:].reshape(ways, -1)[:, :TABLE]
    picked = [lax.dynamic_slice_in_dim(tables, owner[b], 1, 0).reshape(TABLE) for b in range(NB)]
    all_tables = jnp.concatenate(
        [jnp.concatenate(picked).astype(jnp.int32), table.reshape(TABLE)]
    )

    return pl.pallas_call(
        assimilate,
        in_specs=[pl.BlockSpec(memory_space=pltpu.SMEM)] + [vmem] * 4,
        out_specs=vmem,
        out_shape=jax.ShapeDtypeStruct((M, REGION), jnp.bfloat16),
        scratch_shapes=[
            pltpu.VMEM(((NB + 1) * REGION, M), jnp.float32),
            pltpu.VMEM((2 * BLK, M), jnp.float32),
            pltpu.VMEM((NOB // 2 * SPAN, PAIR), jnp.float32),
            pltpu.VMEM((REGION, M), jnp.float32),
            pltpu.VMEM((REGION, M), jnp.float32),
            pltpu.VMEM((NOB, M, M), jnp.bfloat16),
            pltpu.VMEM((BLK, M), jnp.bfloat16),
        ],
        compiler_params=pltpu.CompilerParams(vmem_limit_bytes=40 << 20),
        name="assimilate",
    )(all_tables, owned, mine, rhs, weight)


def solution(mesh):
    placed = (
        P("st", "grp"),
        P("grp", None),
        P("grp", None),
        P("grp", None, None),
        P("grp"),
        P("grp", None),
        P(None, ("grp", "st")),
        P(None, ("grp", "st"), None),
        P(None, ("grp", "st"), None),
    )
    return jax.shard_map(
        shards, mesh=mesh, in_specs=placed, out_specs=P(None, ("grp", "st")), check_vma=False
    )
```

```python
import functools
import math

import jax
import jax.numpy as jnp
from jax import lax
from jax.experimental import pallas as pl
from jax.experimental.pallas import tpu as pltpu
from jax.sharding import PartitionSpec as P

M = 128
BLK = 256
NB = 4
KMAX = 4
SPAN = 64
PAIR = 2 * SPAN
REGION = 1024
BLOCKS = REGION // BLK
NOB = REGION // SPAN
ENTRY = 1 + 2 * KMAX
TABLE = NB * BLOCKS * ENTRY
ROOT = math.sqrt(M - 1.0)
inflation = 4.0
NN = (((1,), (0,)), ((), ()))
MESH = pl.DeviceIdType.MESH
NT = (((1,), (1,)), ((), ()))


def split(x):
    high = x.astype(jnp.bfloat16)
    return high, (x - high.astype(jnp.float32)).astype(jnp.bfloat16)


def dot3(x, y, dims):
    def one(a, b):
        return lax.dot_general(a, b, dims, preferred_element_type=jnp.float32)

    return one(x[0], y[0]) + (one(x[0], y[1]) + one(x[1], y[0]))


def exchange(ways, value_ref, spread_ref, local_ref, noise_ref, sent_ref, share_ref,
             got_ref, mine_ref, rhs_ref, weight_ref, send_sem, recv_sem, part_send, part_recv):
    me = lax.axis_index("st")
    partner = me + 1 - 2 * lax.rem(me, 2)
    half = ways // 2

    barrier = pltpu.get_barrier_semaphore()

    def greet(step, carry):
        peer = lax.rem(me + step, ways)
        pl.semaphore_signal(barrier, inc=1, device_id={"st": peer}, device_id_type=MESH)
        return carry

    lax.fori_loop(1, ways, greet, 0)
    pl.semaphore_wait(barrier, ways - 1)

    def whole(step):
        peer = lax.rem(me + 2 * step, ways)
        return pltpu.make_async_remote_copy(
            src_ref=sent_ref, dst_ref=got_ref.at[me], send_sem=send_sem.at[step],
            recv_sem=recv_sem.at[me], device_id={"st": peer}, device_id_type=MESH)

    def across(source, slot, src_ref):
        return pltpu.make_async_remote_copy(
            src_ref=src_ref, dst_ref=got_ref.at[source], send_sem=send_sem.at[slot],
            recv_sem=recv_sem.at[source], device_id={"st": partner}, device_id_type=MESH)

    def part(step):
        peer = lax.rem(me + step, ways)
        return pltpu.make_async_remote_copy(
            src_ref=share_ref.at[peer], dst_ref=mine_ref.at[me], send_sem=part_send.at[step],
            recv_sem=part_recv.at[me], device_id={"st": peer}, device_id_type=MESH)

    def arrived(source):
        pltpu.make_async_remote_copy(
            src_ref=sent_ref, dst_ref=got_ref.at[source], send_sem=send_sem.at[0],
            recv_sem=recv_sem.at[source], device_id={"st": partner}, device_id_type=MESH).wait_recv()

    def loop(low, high, body):
        lax.fori_loop(low, high, lambda i, c: (body(i), c)[1], 0)

    loop(1, half, lambda step: whole(step).start())
    across(me, 0, sent_ref).start()
    loop(1, ways, lambda step: part(step).start())
    got_ref[me] = sent_ref[...]
    mine_ref[me] = share_ref[me]

    def one(batch, k):
        cols = pl.ds(pl.multiple_of(k * BLK, BLK), BLK)
        inv = 1.0 / (math.sqrt(inflation) * spread_ref[batch, :, cols])
        var = lax.broadcasted_iota(jnp.int32, (SPAN, BLK), 0) + k * SPAN
        hit = var == local_ref[batch, :, cols]
        placed = jnp.where(hit, inv, 0.0)
        high = placed.astype(jnp.bfloat16)
        low = (placed - high.astype(jnp.float32)).astype(jnp.bfloat16)
        noise = noise_ref[batch, :, cols]
        summed = lax.dot_general(high, noise, NT, preferred_element_type=jnp.float32)
        summed += lax.dot_general(low, noise, NT, preferred_element_type=jnp.float32)
        square = placed * inv
        weight = jnp.sum(square, axis=1, keepdims=True)
        summed += jnp.sum(square * value_ref[batch, :, cols], axis=1, keepdims=True)
        rows = pl.ds(pl.multiple_of(k * SPAN, SPAN), SPAN)
        rhs_ref[batch, rows, :] = summed
        weight_ref[batch, rows, :] = jnp.broadcast_to(weight, (SPAN, M))

    def two(i, batch):
        one(batch, 2 * i)
        one(batch, 2 * i + 1)

    for batch in range(NB):
        loop(0, NOB // 2, lambda i: two(i, batch))

    def pass_on(step):
        source = lax.rem(me + ways - 2 * step, ways)
        arrived(source)
        across(source, half + step, got_ref.at[source]).start()

    loop(1, half, pass_on)

    def passed(step):
        arrived(lax.rem(partner + ways - 2 * step, ways))

    loop(0, half, passed)

    def settle(step):
        whole(step).wait_send()
        across(me, half + step, sent_ref).wait_send()

    loop(1, half, settle)
    across(me, 0, sent_ref).wait_send()

    def parted(step):
        part(step).wait_send()
        source = lax.rem(me + ways - step, ways)
        pltpu.make_async_remote_copy(
            src_ref=share_ref.at[me], dst_ref=mine_ref.at[source], send_sem=part_send.at[0],
            recv_sem=part_recv.at[source], device_id={"st": partner}, device_id_type=MESH).wait_recv()

    loop(1, ways, parted)


def assimilate(table_ref, owned_ref, mine_ref, rhs_ref, weight_ref, out_ref,
               state, taper, system, right, factor, weights, anoms):
    lane = lax.broadcasted_iota(jnp.int32, (SPAN, PAIR), 1)
    first = lane < SPAN
    chunks = REGION // 128

    def bring_owned(c, carry):
        at = pl.multiple_of(c * 128, 128)
        state[pl.ds(at, 128), :] = owned_ref[:, pl.ds(at, 128)].astype(jnp.float32).T
        return carry

    lax.fori_loop(0, NB * chunks, bring_owned, 0, unroll=4)

    def bring_mine(c, carry):
        at = pl.multiple_of(c * 128, 128)
        state[pl.ds(NB * REGION + at, 128), :] = mine_ref[:, pl.ds(at, 128)].astype(jnp.float32).T
        return carry

    lax.fori_loop(0, chunks, bring_mine, 0, unroll=4)

    offset = (lax.broadcasted_iota(jnp.int32, (2 * BLK, M), 0) - BLK).astype(jnp.float32)
    ratio = offset / (BLK / 4.0)
    taper[...] = 1.0 / (1.0 + ratio * ratio)

    for batch in range(NB):

        def build(p, carry):
            rows = pl.ds(pl.multiple_of(p * PAIR, PAIR), PAIR)
            x = state[pl.ds(pl.multiple_of(batch * REGION + p * PAIR, PAIR), PAIR), :]
            anom = x - jnp.mean(x, axis=1, keepdims=True)
            weight = weight_ref[batch, rows, :]
            live = weight > 0.0
            inverse = jnp.where(live, lax.rsqrt(jnp.where(live, weight, 1.0)), 0.0)
            scaled = anom * (weight * inverse * (1.0 / ROOT))
            factor[rows, :] = scaled
            right[rows, :] = (rhs_ref[batch, rows, :] - weight * x) * (inverse * (1.0 / ROOT))
            pieces = split(scaled)
            gram = dot3(pieces, pieces, NT)
            row = lax.broadcasted_iota(jnp.int32, (SPAN, PAIR), 0)
            eye = jnp.where(row == jnp.where(first, lane, lane - SPAN), 1.0, 0.0)
            packed = jnp.where(first, gram[:SPAN], gram[SPAN:]) + eye
            system[pl.ds(pl.multiple_of(p * SPAN, SPAN), SPAN), :] = packed
            return carry

        lax.fori_loop(0, NOB // 2, build, 0, unroll=8)

        def eliminate(j, carry):
            pick = jnp.where(first, j, j + SPAN)
            hit = lane == pick
            pairs = range(NOB // 2)
            fulls = [system[p * SPAN:(p + 1) * SPAN, :] for p in pairs]
            rows = system[pl.ds(j, NOB // 2, stride=SPAN), :]
            inv = 1.0 / jnp.take_along_axis(rows, pick[:NOB // 2], axis=1)
            scaled = jnp.where(hit[:NOB // 2], inv, rows * inv)
            columns = [jnp.take_along_axis(full, pick, axis=1) for full in fulls]
            made = [
                jnp.where(hit, 0.0, fulls[p]) - columns[p] * scaled[p:p + 1] for p in pairs
            ]
            for p in pairs:
                system[p * SPAN:(p + 1) * SPAN, :] = made[p]
            system[pl.ds(j, NOB // 2, stride=SPAN), :] = scaled
            return carry

        lax.fori_loop(0, SPAN, eliminate, 0)

        def finish(p, carry):
            rows = pl.ds(pl.multiple_of(p * PAIR, PAIR), PAIR)
            packed = system[pl.ds(pl.multiple_of(p * SPAN, SPAN), SPAN), :]
            whole = jnp.concatenate([jnp.where(first, packed, 0.0), jnp.where(first, 0.0, packed)], axis=0)
            solved = split(dot3(split(whole), split(right[rows, :]), NN))
            left = factor[rows, :].T
            lanes = lax.broadcasted_iota(jnp.int32, (M, PAIR), 1) < SPAN
            for half, keep in enumerate((lanes, jnp.logical_not(lanes))):
                made = dot3(split(jnp.where(keep, left, 0.0)), solved, NN)
                weights[2 * p + half] = made.astype(jnp.bfloat16)
            return carry

        lax.fori_loop(0, NOB // 2, finish, 0, unroll=8)

        def update(index, carry):
            region = batch + 1 + index
            blocks = range(BLOCKS)
            bases = [((region * NB + batch) * BLOCKS + i) * ENTRY for i in blocks]
            rows = [pl.ds(pl.multiple_of(region * REGION + i * BLK, BLK), BLK) for i in blocks]

            def term(i, j, anom):
                k = table_ref[bases[i] + 1 + j]
                shift = table_ref[bases[i] + 1 + KMAX + j]
                made = jnp.dot(anom, weights[k], preferred_element_type=jnp.float32)
                return made * taper[pl.ds(BLK - shift, BLK), :]

            for i in blocks:
                x = state[rows[i], :]
                anom = (x - jnp.mean(x, axis=1, keepdims=True)).astype(jnp.bfloat16)
                anoms[i] = anom
                state[rows[i], :] = x + term(i, 0, anom)

            for i in blocks:

                def slot(j, carry):
                    state[rows[i], :] += term(i, j, anoms[i])
                    return carry

                lax.fori_loop(1, table_ref[bases[i]], slot, 0)
            return carry

        lax.fori_loop(0, NB - batch, update, 0)

    def leave(c, carry):
        at = pl.multiple_of(c * 128, 128)
        out_ref[:, pl.ds(at, 128)] = state[pl.ds(NB * REGION + at, 128), :].T.astype(jnp.bfloat16)
        return carry

    lax.fori_loop(0, chunks, leave, 0, unroll=4)


def shards(
    ensemble, obs_value, obs_spread, obs_noise, owner, obs_local, loc_count, loc_obs, loc_shift
):
    members = ensemble.shape[0]
    ways = M // members
    table = jnp.concatenate([loc_count[:, :, None], loc_obs, loc_shift], axis=2)
    wide = REGION // 128
    base = NB * wide * members
    total = -(-(base + -(-TABLE // 128)) // 16) * 16
    flat = jnp.pad(table.reshape(TABLE).astype(jnp.bfloat16), (0, (total - base) * 128 - TABLE))

    def tall(x):
        return x.reshape(members, -1, 128).transpose(1, 0, 2).reshape(-1, 128)

    parts = [tall(lax.dynamic_slice_in_dim(ensemble, owner[b] * REGION, REGION, 1)) for b in range(NB)]
    sent = jnp.concatenate(parts + [flat.reshape(total - base, 128)], axis=0)
    share = tall(ensemble).reshape(ways, wide * members, 128)
    held = -(-wide * members // 16) * 16
    share = jnp.pad(share, ((0, 0), (0, held - wide * members), (0, 0)))

    vmem = pl.BlockSpec(memory_space=pltpu.VMEM)
    sums = jax.ShapeDtypeStruct((NB, REGION, M), jnp.float32)
    got, mine, rhs, weight = pl.pallas_call(
        functools.partial(exchange, ways),
        in_specs=[vmem] * 6,
        out_specs=[vmem] * 4,
        out_shape=[
            jax.ShapeDtypeStruct((ways, total, 128), jnp.bfloat16),
            jax.ShapeDtypeStruct((ways, held, 128), jnp.bfloat16),
            sums,
            sums,
        ],
        scratch_shapes=[pltpu.SemaphoreType.DMA((ways,))] * 4,
        compiler_params=pltpu.CompilerParams(
            collective_id=0, has_side_effects=True, vmem_limit_bytes=40 << 20
        ),
        name="exchange",
    )(obs_value[:, None], obs_spread[:, None], obs_local[:, None], obs_noise, sent, share)

    def across(x, count):
        return x[:, :count * members].reshape(ways, count, members, 128).transpose(0, 2, 1, 3).reshape(M, count * 128)

    owned = across(got, NB * wide)
    mine = across(mine, wide)
    tables = got[:, base:].reshape(ways, -1)[:, :TABLE]
    picked = [lax.dynamic_slice_in_dim(tables, owner[b], 1, 0).reshape(TABLE) for b in range(NB)]
    all_tables = jnp.concatenate(
        [jnp.concatenate(picked).astype(jnp.int32), table.reshape(TABLE)]
    )

    return pl.pallas_call(
        assimilate,
        in_specs=[pl.BlockSpec(memory_space=pltpu.SMEM)] + [vmem] * 4,
        out_specs=vmem,
        out_shape=jax.ShapeDtypeStruct((M, REGION), jnp.bfloat16),
        scratch_shapes=[
            pltpu.VMEM(((NB + 1) * REGION, M), jnp.float32),
            pltpu.VMEM((2 * BLK, M), jnp.float32),
            pltpu.VMEM((NOB // 2 * SPAN, PAIR), jnp.float32),
            pltpu.VMEM((REGION, M), jnp.float32),
            pltpu.VMEM((REGION, M), jnp.float32),
            pltpu.VMEM((NOB, M, M), jnp.bfloat16),
            pltpu.VMEM((BLOCKS, BLK, M), jnp.bfloat16),
        ],
        compiler_params=pltpu.CompilerParams(vmem_limit_bytes=40 << 20),
        name="assimilate",
    )(all_tables, owned, mine, rhs, weight)


def solution(mesh):
    placed = (
        P("st", "grp"),
        P("grp", None),
        P("grp", None),
        P("grp", None, None),
        P("grp"),
        P("grp", None),
        P(None, ("grp", "st")),
        P(None, ("grp", "st"), None),
        P(None, ("grp", "st"), None),
    )
    return jax.shard_map(
        shards, mesh=mesh, in_specs=placed, out_specs=P(None, ("grp", "st")), check_vma=False
    )
```

```python
import functools
import math

import jax
import jax.numpy as jnp
from jax import lax
from jax.experimental import pallas as pl
from jax.experimental.pallas import tpu as pltpu
from jax.sharding import PartitionSpec as P

M = 128
BLK = 256
NB = 4
KMAX = 4
SPAN = 64
PAIR = 2 * SPAN
REGION = 1024
BLOCKS = REGION // BLK
NOB = REGION // SPAN
ENTRY = 1 + 2 * KMAX
TABLE = NB * BLOCKS * ENTRY
ROOT = math.sqrt(M - 1.0)
inflation = 4.0
NN = (((1,), (0,)), ((), ()))
MESH = pl.DeviceIdType.MESH
NT = (((1,), (1,)), ((), ()))


def split(x):
    high = x.astype(jnp.bfloat16)
    return high, (x - high.astype(jnp.float32)).astype(jnp.bfloat16)


def dot3(x, y, dims):
    def one(a, b):
        return lax.dot_general(a, b, dims, preferred_element_type=jnp.float32)

    return one(x[0], y[0]) + (one(x[0], y[1]) + one(x[1], y[0]))


def exchange(ways, value_ref, spread_ref, local_ref, noise_ref, sent_ref, share_ref,
             got_ref, mine_ref, rhs_ref, weight_ref, send_sem, recv_sem, part_send, part_recv):
    me = lax.axis_index("st")
    partner = me + 1 - 2 * lax.rem(me, 2)
    half = ways // 2

    barrier = pltpu.get_barrier_semaphore()

    def greet(step, carry):
        peer = lax.rem(me + step, ways)
        pl.semaphore_signal(barrier, inc=1, device_id={"st": peer}, device_id_type=MESH)
        return carry

    lax.fori_loop(1, ways, greet, 0)
    pl.semaphore_wait(barrier, ways - 1)

    def whole(step):
        peer = lax.rem(me + 2 * step, ways)
        return pltpu.make_async_remote_copy(
            src_ref=sent_ref, dst_ref=got_ref.at[me], send_sem=send_sem.at[step],
            recv_sem=recv_sem.at[me], device_id={"st": peer}, device_id_type=MESH)

    def across(source, slot, src_ref):
        return pltpu.make_async_remote_copy(
            src_ref=src_ref, dst_ref=got_ref.at[source], send_sem=send_sem.at[slot],
            recv_sem=recv_sem.at[source], device_id={"st": partner}, device_id_type=MESH)

    def part(step):
        peer = lax.rem(me + step, ways)
        return pltpu.make_async_remote_copy(
            src_ref=share_ref.at[peer], dst_ref=mine_ref.at[me], send_sem=part_send.at[step],
            recv_sem=part_recv.at[me], device_id={"st": peer}, device_id_type=MESH)

    def arrived(source):
        pltpu.make_async_remote_copy(
            src_ref=sent_ref, dst_ref=got_ref.at[source], send_sem=send_sem.at[0],
            recv_sem=recv_sem.at[source], device_id={"st": partner}, device_id_type=MESH).wait_recv()

    def loop(low, high, body):
        lax.fori_loop(low, high, lambda i, c: (body(i), c)[1], 0)

    loop(1, half, lambda step: whole(step).start())
    across(me, 0, sent_ref).start()
    loop(1, ways, lambda step: part(step).start())
    got_ref[me] = sent_ref[...]
    mine_ref[me] = share_ref[me]

    def one(batch, k):
        cols = pl.ds(pl.multiple_of(k * BLK, BLK), BLK)
        inv = 1.0 / (math.sqrt(inflation) * spread_ref[batch, :, cols])
        var = lax.broadcasted_iota(jnp.int32, (SPAN, BLK), 0) + k * SPAN
        hit = var == local_ref[batch, :, cols]
        placed = jnp.where(hit, inv, 0.0)
        high = placed.astype(jnp.bfloat16)
        low = (placed - high.astype(jnp.float32)).astype(jnp.bfloat16)
        noise = noise_ref[batch, :, cols]
        summed = lax.dot_general(high, noise, NT, preferred_element_type=jnp.float32)
        summed += lax.dot_general(low, noise, NT, preferred_element_type=jnp.float32)
        square = placed * inv
        weight = jnp.sum(square, axis=1, keepdims=True)
        summed += jnp.sum(square * value_ref[batch, :, cols], axis=1, keepdims=True)
        rows = pl.ds(pl.multiple_of(k * SPAN, SPAN), SPAN)
        rhs_ref[batch, rows, :] = summed
        weight_ref[batch, rows, :] = jnp.broadcast_to(weight, (SPAN, M))

    def two(i, batch):
        one(batch, 2 * i)
        one(batch, 2 * i + 1)

    for batch in range(NB):
        loop(0, NOB // 2, lambda i: two(i, batch))

    def pass_on(step):
        source = lax.rem(me + ways - 2 * step, ways)
        arrived(source)
        across(source, half + step, got_ref.at[source]).start()

    loop(1, half, pass_on)

    def passed(step):
        arrived(lax.rem(partner + ways - 2 * step, ways))

    loop(0, half, passed)

    def settle(step):
        whole(step).wait_send()
        across(me, half + step, sent_ref).wait_send()

    loop(1, half, settle)
    across(me, 0, sent_ref).wait_send()

    def parted(step):
        part(step).wait_send()
        source = lax.rem(me + ways - step, ways)
        pltpu.make_async_remote_copy(
            src_ref=share_ref.at[me], dst_ref=mine_ref.at[source], send_sem=part_send.at[0],
            recv_sem=part_recv.at[source], device_id={"st": partner}, device_id_type=MESH).wait_recv()

    loop(1, ways, parted)


def pack(owner_ref, share_ref, flat_ref, sent_ref):
    rows = (sent_ref.shape[0] - flat_ref.shape[0]) // NB
    for b in range(NB):
        sent_ref[b * rows:(b + 1) * rows, :] = share_ref[owner_ref[b]][:rows]
    sent_ref[NB * rows:, :] = flat_ref[...]


def assimilate(ways, owner_ref, table_ref, owned_ref, mine_ref, rhs_ref, weight_ref, out_ref,
               state, taper, system, right, factor, weights, anoms):
    lane = lax.broadcasted_iota(jnp.int32, (SPAN, PAIR), 1)
    first = lane < SPAN
    chunks = REGION // 128

    def bring_owned(c, carry):
        at = pl.multiple_of(c * 128, 128)
        state[pl.ds(at, 128), :] = owned_ref[:, pl.ds(at, 128)].astype(jnp.float32).T
        return carry

    lax.fori_loop(0, NB * chunks, bring_owned, 0, unroll=4)

    def bring_mine(c, carry):
        at = pl.multiple_of(c * 128, 128)
        state[pl.ds(NB * REGION + at, 128), :] = mine_ref[:, pl.ds(at, 128)].astype(jnp.float32).T
        return carry

    lax.fori_loop(0, chunks, bring_mine, 0, unroll=4)

    offset = (lax.broadcasted_iota(jnp.int32, (2 * BLK, M), 0) - BLK).astype(jnp.float32)
    ratio = offset / (BLK / 4.0)
    taper[...] = 1.0 / (1.0 + ratio * ratio)

    for batch in range(NB):

        def build(p, carry):
            rows = pl.ds(pl.multiple_of(p * PAIR, PAIR), PAIR)
            x = state[pl.ds(pl.multiple_of(batch * REGION + p * PAIR, PAIR), PAIR), :]
            anom = x - jnp.mean(x, axis=1, keepdims=True)
            weight = weight_ref[batch, rows, :]
            live = weight > 0.0
            inverse = jnp.where(live, lax.rsqrt(jnp.where(live, weight, 1.0)), 0.0)
            scaled = anom * (weight * inverse * (1.0 / ROOT))
            factor[rows, :] = scaled
            right[rows, :] = (rhs_ref[batch, rows, :] - weight * x) * (inverse * (1.0 / ROOT))
            pieces = split(scaled)
            gram = dot3(pieces, pieces, NT)
            row = lax.broadcasted_iota(jnp.int32, (SPAN, PAIR), 0)
            eye = jnp.where(row == jnp.where(first, lane, lane - SPAN), 1.0, 0.0)
            packed = jnp.where(first, gram[:SPAN], gram[SPAN:]) + eye
            system[pl.ds(pl.multiple_of(p * SPAN, SPAN), SPAN), :] = packed
            return carry

        lax.fori_loop(0, NOB // 2, build, 0, unroll=8)

        def eliminate(j, carry):
            pick = jnp.where(first, j, j + SPAN)
            hit = lane == pick
            pairs = range(NOB // 2)
            fulls = [system[p * SPAN:(p + 1) * SPAN, :] for p in pairs]
            rows = system[pl.ds(j, NOB // 2, stride=SPAN), :]
            inv = 1.0 / jnp.take_along_axis(rows, pick[:NOB // 2], axis=1)
            scaled = jnp.where(hit[:NOB // 2], inv, rows * inv)
            columns = [jnp.take_along_axis(full, pick, axis=1) for full in fulls]
            made = [
                jnp.where(hit, 0.0, fulls[p]) - columns[p] * scaled[p:p + 1] for p in pairs
            ]
            for p in pairs:
                system[p * SPAN:(p + 1) * SPAN, :] = made[p]
            system[pl.ds(j, NOB // 2, stride=SPAN), :] = scaled
            return carry

        lax.fori_loop(0, SPAN, eliminate, 0)

        def finish(p, carry):
            rows = pl.ds(pl.multiple_of(p * PAIR, PAIR), PAIR)
            packed = system[pl.ds(pl.multiple_of(p * SPAN, SPAN), SPAN), :]
            whole = jnp.concatenate([jnp.where(first, packed, 0.0), jnp.where(first, 0.0, packed)], axis=0)
            solved = split(dot3(split(whole), split(right[rows, :]), NN))
            left = factor[rows, :].T
            lanes = lax.broadcasted_iota(jnp.int32, (M, PAIR), 1) < SPAN
            for half, keep in enumerate((lanes, jnp.logical_not(lanes))):
                made = dot3(split(jnp.where(keep, left, 0.0)), solved, NN)
                weights[2 * p + half] = made.astype(jnp.bfloat16)
            return carry

        lax.fori_loop(0, NOB // 2, finish, 0, unroll=8)

        def update(index, carry):
            region = batch + 1 + index
            blocks = range(BLOCKS)
            place = jnp.where(region == NB, ways, owner_ref[jnp.minimum(region, NB - 1)])
            bases = [place * TABLE + (batch * BLOCKS + i) * ENTRY for i in blocks]
            rows = [pl.ds(pl.multiple_of(region * REGION + i * BLK, BLK), BLK) for i in blocks]

            def term(i, j, anom):
                k = table_ref[bases[i] + 1 + j]
                shift = table_ref[bases[i] + 1 + KMAX + j]
                made = jnp.dot(anom, weights[k], preferred_element_type=jnp.float32)
                return made * taper[pl.ds(BLK - shift, BLK), :]

            for i in blocks:
                x = state[rows[i], :]
                anom = (x - jnp.mean(x, axis=1, keepdims=True)).astype(jnp.bfloat16)
                anoms[i] = anom
                state[rows[i], :] = x + term(i, 0, anom)

            for i in blocks:

                def slot(j, carry):
                    state[rows[i], :] += term(i, j, anoms[i])
                    return carry

                lax.fori_loop(1, table_ref[bases[i]], slot, 0)
            return carry

        lax.fori_loop(0, NB - batch, update, 0)

    def leave(c, carry):
        at = pl.multiple_of(c * 128, 128)
        out_ref[:, pl.ds(at, 128)] = state[pl.ds(NB * REGION + at, 128), :].T.astype(jnp.bfloat16)
        return carry

    lax.fori_loop(0, chunks, leave, 0, unroll=4)


def shards(
    ensemble, obs_value, obs_spread, obs_noise, owner, obs_local, loc_count, loc_obs, loc_shift
):
    members = ensemble.shape[0]
    ways = M // members
    table = jnp.concatenate([loc_count[:, :, None], loc_obs, loc_shift], axis=2)
    wide = REGION // 128
    base = NB * wide * members
    total = -(-(base + -(-TABLE // 128)) // 16) * 16
    flat = jnp.pad(table.reshape(TABLE).astype(jnp.bfloat16), (0, (total - base) * 128 - TABLE))

    def tall(x):
        return x.reshape(members, -1, 128).transpose(1, 0, 2).reshape(-1, 128)

    share = tall(ensemble).reshape(ways, wide * members, 128)
    held = -(-wide * members // 16) * 16
    share = jnp.pad(share, ((0, 0), (0, held - wide * members), (0, 0)))

    vmem = pl.BlockSpec(memory_space=pltpu.VMEM)
    smem = pl.BlockSpec(memory_space=pltpu.SMEM)
    sent = pl.pallas_call(
        pack,
        in_specs=[smem, vmem, vmem],
        out_specs=vmem,
        out_shape=jax.ShapeDtypeStruct((total, 128), jnp.bfloat16),
        compiler_params=pltpu.CompilerParams(vmem_limit_bytes=16 << 20),
        name="pack",
    )(owner, share, flat.reshape(total - base, 128))
    sums = jax.ShapeDtypeStruct((NB, REGION, M), jnp.float32)
    got, mine, rhs, weight = pl.pallas_call(
        functools.partial(exchange, ways),
        in_specs=[vmem] * 6,
        out_specs=[vmem] * 4,
        out_shape=[
            jax.ShapeDtypeStruct((ways, total, 128), jnp.bfloat16),
            jax.ShapeDtypeStruct((ways, held, 128), jnp.bfloat16),
            sums,
            sums,
        ],
        scratch_shapes=[pltpu.SemaphoreType.DMA((ways,))] * 4,
        compiler_params=pltpu.CompilerParams(
            collective_id=0, has_side_effects=True, vmem_limit_bytes=40 << 20
        ),
        name="exchange",
    )(obs_value[:, None], obs_spread[:, None], obs_local[:, None], obs_noise, sent, share)

    def across(x, count):
        return x[:, :count * members].reshape(ways, count, members, 128).transpose(0, 2, 1, 3).reshape(M, count * 128)

    owned = across(got, NB * wide)
    mine = across(mine, wide)
    tables = got[:, base:].reshape(ways, -1)[:, :TABLE]
    all_tables = jnp.concatenate([tables.astype(jnp.int32).reshape(-1), table.reshape(TABLE)])

    return pl.pallas_call(
        functools.partial(assimilate, ways),
        in_specs=[smem, smem] + [vmem] * 4,
        out_specs=vmem,
        out_shape=jax.ShapeDtypeStruct((M, REGION), jnp.bfloat16),
        scratch_shapes=[
            pltpu.VMEM(((NB + 1) * REGION, M), jnp.float32),
            pltpu.VMEM((2 * BLK, M), jnp.float32),
            pltpu.VMEM((NOB // 2 * SPAN, PAIR), jnp.float32),
            pltpu.VMEM((REGION, M), jnp.float32),
            pltpu.VMEM((REGION, M), jnp.float32),
            pltpu.VMEM((NOB, M, M), jnp.bfloat16),
            pltpu.VMEM((BLOCKS, BLK, M), jnp.bfloat16),
        ],
        compiler_params=pltpu.CompilerParams(vmem_limit_bytes=40 << 20),
        name="assimilate",
    )(owner, all_tables, owned, mine, rhs, weight)


def solution(mesh):
    placed = (
        P("st", "grp"),
        P("grp", None),
        P("grp", None),
        P("grp", None, None),
        P("grp"),
        P("grp", None),
        P(None, ("grp", "st")),
        P(None, ("grp", "st"), None),
        P(None, ("grp", "st"), None),
    )
    return jax.shard_map(
        shards, mesh=mesh, in_specs=placed, out_specs=P(None, ("grp", "st")), check_vma=False
    )
```
